32 devices in a mesh: tm: 4 (over y, x), space: 8 (over z, core).
Axes of the slice: x: 2, y: 2, z: 4, core: 2. Of those that a mesh axis runs over, the one named last changes fastest.
Arguments:
- speed_sq: float32 [32, 256, 256], P('space'), may hold values from 0.04 to 0.3
- misfit_weight: float32 [32, 256, 256], P('space'), may hold values from 0.1 to 1
- checkpoints: float32 [4, 2, 32, 256, 256], P('tm', None, 'space'), may hold values from -6 to 6
- adjoint_final: float32 [2, 32, 256, 256], P(None, 'space'), may hold values from -6 to 6
- slab_steps: int32 [4], replicated, may hold values from 1 to 6, as said below
- restart_group: int32 [4], replicated, may hold values from 0 to 3, as said below
Outputs:
- gradient_image: float32 [32, 256, 256], P('space')
- adjoint_start: float32 [4, 2, 32, 256, 256], P('tm', None, 'space')
The draws below stay inside these ranges and needn't reach their ends.
Inputs may be any that keep to these rules, and one draw needn't show every extreme that they name: `slab_steps`: one slab has exactly 6 steps. `restart_group`: each group is named once.
All inputs are finite; a program needn't handle non-finite values.
Results may differ from the reference program's by a relative error of at most 0.00002.
Values sent between devices are 32-bit elements; how exact they have to be, the bound alone decides.
A program may use at most 128 MiB of HBM per device.

```python
import math
import jax
import jax.numpy as jnp
from jax import lax

NY = 256
NZ = 256
SLAB_MAX = 6
NX = 32
N_TM = 4


def draw_slab_steps(key, part):
    first_key, second_key = jax.random.split(jax.random.fold_in(key, 11))
    lengths_drawn = jax.random.randint(first_key, (N_TM,), 1, SLAB_MAX + 1)
    longest_at = jax.random.randint(second_key, (), 0, N_TM)
    positions = jnp.arange(N_TM)
    return jnp.where(positions == longest_at, SLAB_MAX, lengths_drawn).astype(jnp.int32)


def draw_restart_group(key, part):
    first_key, second_key = jax.random.split(jax.random.fold_in(key, 23))
    shuffled = jax.random.permutation(first_key, N_TM).astype(jnp.int32)
    chosen_at = jax.random.randint(second_key, (), 0, N_TM).astype(jnp.int32)
    target_at = (chosen_at + N_TM // 2) % N_TM
    positions = jnp.arange(N_TM).astype(jnp.int32)
    spot_at = jnp.argmax(shuffled == target_at).astype(jnp.int32)
    held_value = jnp.sum(jnp.where(positions == chosen_at, shuffled, 0))
    result = jnp.where(positions == chosen_at, target_at, jnp.where(positions == spot_at, held_value, shuffled))
    return result.astype(jnp.int32)


def levels(key, extent, cuts, low, largest):
    level = 1.0
    for axis_at, parts in cuts:
        heights = jax.random.uniform(jax.random.fold_in(jax.random.fold_in(key, 6), axis_at), (parts,), jnp.float32, low / len(cuts), largest / len(cuts))
        level = level * jnp.repeat(jnp.exp(heights), extent[axis_at] // parts).reshape((-1,) + (1,) * (len(extent) - 1 - axis_at))
    return level


def centred(own_key, extent, width, most, cuts=(), dtype=jnp.bfloat16):
    values = jax.random.normal(own_key, extent, jnp.float32) * width
    if len(cuts) > 0:
        values = levels(own_key, extent, cuts, -0.22, 0.18) * values
    return jnp.clip(values, min=-most, max=most).astype(dtype)


def setup_inputs(seed: int = 0) -> dict:
    keys = jax.random.split(jax.random.key(seed), 7)
    speed_sq = jnp.clip(jnp.exp(math.log(0.3) - 2.014903 * jax.random.uniform(keys[0], (NX, NY, NZ), jnp.float32) ** levels(keys[0], (NX, NY, NZ), ((0, 8),), -0.2, 0.2)), 0.04, 0.3)
    misfit_weight = jnp.clip(jnp.exp(math.log(1.0) - 2.3025851 * jax.random.uniform(keys[1], (NX, NY, NZ), jnp.float32) ** levels(keys[1], (NX, NY, NZ), ((0, 8),), -0.2, 0.2)), 0.1, 1.0)
    checkpoints = centred(keys[2], (N_TM, 2, NX, NY, NZ), 1.0, 6.0, ((0, 4), (2, 8)), jnp.float32)
    adjoint_final = centred(keys[3], (2, NX, NY, NZ), 1.0, 6.0, ((1, 8),), jnp.float32)
    slab_steps = draw_slab_steps(jax.random.fold_in(keys[6], 71), 0)
    restart_group = draw_restart_group(jax.random.fold_in(keys[6], 71), 0)
    return dict(speed_sq=speed_sq, misfit_weight=misfit_weight, checkpoints=checkpoints, adjoint_final=adjoint_final, slab_steps=slab_steps, restart_group=restart_group)


def yz_sum(center):
    padded = jnp.pad(center, ((0, 0), (1, 1), (1, 1)))
    return padded[:, 2:, 1:-1] + padded[:, :-2, 1:-1] + padded[:, 1:-1, 2:] + padded[:, 1:-1, :-2]


def lap_padded(padded):
    center = padded[1:-1]
    return padded[2:] + padded[:-2] + yz_sum(center) - 6.0 * center


def lap_full(field):
    return lap_padded(jnp.pad(field, ((1, 1), (0, 0), (0, 0))))


def forward(previous, current, speed):
    fields = [current]
    laplaces = []
    for step_at in range(SLAB_MAX):
        laplace = lap_full(current)
        following = 2.0 * current - previous + speed * laplace
        laplaces.append(laplace)
        fields.append(following)
        previous, current = current, following
    return jnp.stack(fields), jnp.stack(laplaces)


def adjoint(fields, laplaces, speed, weight, length, adj_now, adj_next):
    def one_step(turn_step, carry):
        adj_now, adj_next, image = carry
        step_at = length - turn_step
        active = step_at >= 1
        field_now = lax.dynamic_index_in_dim(fields, jnp.clip(step_at, 0, SLAB_MAX).astype(jnp.int32), 0, keepdims=False)
        lap_before = lax.dynamic_index_in_dim(laplaces, jnp.clip(step_at - 1, 0, SLAB_MAX - 1).astype(jnp.int32), 0, keepdims=False)
        adj_prev = 2.0 * adj_now - adj_next + lap_full(speed * adj_now) + weight * field_now
        image = image + jnp.where(active, adj_now * lap_before, jnp.zeros_like(adj_now))
        return (jnp.where(active, adj_prev, adj_now), jnp.where(active, adj_now, adj_next), image)

    return lax.fori_loop(0, SLAB_MAX, one_step, (adj_now, adj_next, jnp.zeros_like(adj_now)))


def reference(speed_sq, misfit_weight, checkpoints, adjoint_final, slab_steps, restart_group):
    image = jnp.zeros_like(speed_sq)
    adj_now, adj_next = adjoint_final[0], adjoint_final[1]
    starts = [None] * N_TM
    for group in reversed(range(N_TM)):
        restart = lax.dynamic_index_in_dim(checkpoints, restart_group[group].astype(jnp.int32), 0, keepdims=False)
        fields, laplaces = forward(restart[0], restart[1], speed_sq)
        adj_now, adj_next, part = adjoint(fields, laplaces, speed_sq, misfit_weight, slab_steps[group], adj_now, adj_next)
        image = image + part
        starts[group] = jnp.stack([adj_now, adj_next])
    return image, jnp.stack(starts)
```

```python
import functools

import jax
import jax.numpy as jnp
from jax import lax
from jax.experimental import pallas as pl
from jax.experimental.pallas import tpu as pltpu
from jax.sharding import PartitionSpec as P

SLAB_MAX = 6
CHUNK = 32
EDGE = 8


def kernel(steps, tab, speed_h, weight_h, ck_h, af_h, img_o, st_o,
           ck, u, laps, s, hist, image, spd, wgt, stage,
           load_sem, ck_send, ck_recv, f_send, f_recv, a_send, a_recv,
           st_send, st_recv, im_send, im_recv):
    groups = st_recv.shape[0]
    planes, rows, _ = spd.shape
    me = lax.axis_index("tm")
    sp = lax.axis_index("space")
    n_tm = lax.axis_size("tm")
    n_sp = lax.axis_size("space")

    def place(m):
        return m + (m // 2) * (1 - 2 * (m % 2))

    q = place(me)
    inner = pl.ds(EDGE, rows)
    span = pl.ds(1, planes)
    partners = [lax.rem(me + d, n_tm) for d in range(1, n_tm)]
    has = [sp > 0, sp < n_sp - 1, q > 0, q < n_tm - 1]
    opposite = [1, 0, 3, 2]
    target = [{"space": jnp.maximum(sp - 1, 0)}, {"space": jnp.minimum(sp + 1, n_sp - 1)},
              {"tm": place(jnp.maximum(q - 1, 0))}, {"tm": place(jnp.minimum(q + 1, n_tm - 1))}]

    def halo(d, ref, at, send, recv):
        if d == 0:
            src, dst = ref.at[at, 1, inner, :], ref.at[at, planes + 1, inner, :]
        elif d == 1:
            src, dst = ref.at[at, planes, inner, :], ref.at[at, 0, inner, :]
        elif d == 2:
            src, dst = ref.at[at, span, pl.ds(EDGE, EDGE), :], ref.at[at, span, pl.ds(EDGE + rows, EDGE), :]
        else:
            src, dst = ref.at[at, span, pl.ds(rows, EDGE), :], ref.at[at, span, pl.ds(0, EDGE), :]
        return pltpu.make_async_remote_copy(
            src_ref=src, dst_ref=dst, send_sem=send, recv_sem=recv,
            device_id=target[d], device_id_type=pl.DeviceIdType.MESH)

    def start(dirs, ref, at, sems):
        for d in dirs:
            @pl.when(has[d])
            def _():
                halo(d, ref, at, sems[0](d), sems[1](d)).start()

    def finish(ref, at, sems):
        for d in range(4):
            @pl.when(has[opposite[d]])
            def _():
                halo(d, ref, at, sems[0](d), sems[1](d)).wait_recv()
        for d in range(4):
            @pl.when(has[d])
            def _():
                halo(d, ref, at, sems[0](d), sems[1](d)).wait_send()

    mine = pl.ds(pl.multiple_of(q * rows, rows), rows)
    loads = [
        pltpu.make_async_copy(speed_h.at[:, mine, :], spd, load_sem.at[0]),
        pltpu.make_async_copy(weight_h.at[:, mine, :], wgt, load_sem.at[1]),
        pltpu.make_async_copy(af_h.at[0, :, mine, :], hist.at[1], load_sem.at[2]),
        pltpu.make_async_copy(af_h.at[1, :, mine, :], hist.at[0], load_sem.at[3]),
        pltpu.make_async_copy(ck_h.at[0, :, :, mine, :], ck.at[me], load_sem.at[4]),
    ]
    for one in loads:
        one.start()

    barrier = pltpu.get_barrier_semaphore()
    for m in partners:
        pl.semaphore_signal(barrier, inc=1, device_id={"tm": m}, device_id_type=pl.DeviceIdType.MESH)
    for d in range(2):
        @pl.when(has[d])
        def _():
            pl.semaphore_signal(barrier, inc=1, device_id=target[d], device_id_type=pl.DeviceIdType.MESH)
    peers = len(partners) + has[0].astype(jnp.int32) + has[1].astype(jnp.int32)
    pl.semaphore_wait(barrier, peers)

    def ck_copy(i):
        m = partners[i]
        theirs = pl.ds(pl.multiple_of(place(m) * rows, rows), rows)
        return pltpu.make_async_remote_copy(
            src_ref=ck_h.at[0, :, :, theirs, :], dst_ref=ck.at[me],
            send_sem=ck_send.at[i], recv_sem=ck_recv.at[i],
            device_id={"tm": m}, device_id_type=pl.DeviceIdType.MESH)

    for i in range(len(partners)):
        ck_copy(i).start()

    line = jnp.zeros((rows, spd.shape[2]), jnp.float32)
    band = jnp.zeros((EDGE, spd.shape[2]), jnp.float32)
    for ref in (u, s):
        for d, p in ((0, 0), (1, planes + 1)):
            @pl.when(jnp.logical_not(has[d]))
            def _():
                def clear(i, c):
                    ref[i, p, EDGE:EDGE + rows, :] = line
                    return c
                lax.fori_loop(0, ref.shape[0], clear, 0)
        for d, r in ((2, 0), (3, EDGE + rows)):
            @pl.when(jnp.logical_not(has[d]))
            def _():
                def clear(i, c):
                    for p in range(planes):
                        ref[i, 1 + p, r:r + EDGE, :] = band
                    return c
                lax.fori_loop(0, ref.shape[0], clear, 0)
    blank = laps.shape[0] - 1
    for p in range(planes):
        laps[blank, p] = line
        image[p] = line

    lane = lax.broadcasted_iota(jnp.int32, (CHUNK, spd.shape[2]), 1)
    first = lane == 0
    last = lane == spd.shape[2] - 1
    zero = jnp.zeros((CHUNK, spd.shape[2]), jnp.float32)

    def lap(ref, at, p, r):
        c = ref[at, p + 1, EDGE + r:EDGE + r + CHUNK, :]
        total = ref[at, p, EDGE + r:EDGE + r + CHUNK, :] + ref[at, p + 2, EDGE + r:EDGE + r + CHUNK, :]
        total += ref[at, p + 1, EDGE + r - 1:EDGE + r - 1 + CHUNK, :]
        total += ref[at, p + 1, EDGE + r + 1:EDGE + r + 1 + CHUNK, :]
        total += jnp.where(first, zero, pltpu.roll(c, 1, 1))
        total += jnp.where(last, zero, pltpu.roll(c, c.shape[1] - 1, 1))
        return c, total - 6.0 * c

    for one in loads:
        one.wait()

    def a_sems(par):
        return (lambda d: a_send.at[par, d]), (lambda d: a_recv.at[par, d])

    def f_sems(par, g):
        return (lambda d: f_send.at[par, g, d]), (lambda d: f_recv.at[par, g, d])

    for p in range(planes):
        s[0, 1 + p, EDGE:EDGE + rows, :] = spd[p] * hist[1, p]

    for i in range(len(partners)):
        ck_copy(i).wait_recv()
    for g in range(groups):
        source = tab[2 * steps + g]
        for p in range(planes):
            u[groups + g, 1 + p, EDGE:EDGE + rows, :] = ck[source, 1, p]
        start(range(4), u, groups + g, f_sems(0, g))
        for p in range(planes):
            u[g, 1 + p, EDGE:EDGE + rows, :] = ck[source, 0, p]
    start(range(4), s, 0, a_sems(0))

    order = (0, planes - 1) + tuple(range(1, planes - 1))

    def forward(n, carry):
        par, later = lax.rem(n, 2), lax.rem(n + 1, 2)
        for g in range(groups):
            at = (n + 1) * groups + g
            finish(u, at, f_sems(par, g))
            for k, p in enumerate(order):
                for r in range(0, rows, CHUNK):
                    here = slice(EDGE + r, EDGE + r + CHUNK)
                    c, laplace = lap(u, at, p, r)
                    laps[n * groups + g, p, r:r + CHUNK, :] = laplace
                    u[at + groups, 1 + p, here, :] = (
                        2.0 * c - u[at - groups, 1 + p, here, :] + spd[p, r:r + CHUNK, :] * laplace)
                if k == 1:
                    @pl.when(n < SLAB_MAX - 1)
                    def _():
                        start((0, 1), u, at + groups, f_sems(later, g))

            @pl.when(n < SLAB_MAX - 1)
            def _():
                start((2, 3), u, at + groups, f_sems(later, g))
        return carry

    lax.fori_loop(0, SLAB_MAX, forward, 0)

    def adjoint(t, carry):
        par, later = lax.rem(t, 2), lax.rem(t + 1, 2)
        at_u, at_lap = tab[t], tab[steps + t]
        finish(s, par, a_sems(par))
        for k, p in enumerate(order):
            for r in range(0, rows, CHUNK):
                here = slice(r, r + CHUNK)
                pad = slice(EDGE + r, EDGE + r + CHUNK)
                _, laplace = lap(s, par, p, r)
                new = (2.0 * hist[t + 1, p, here, :] - hist[t, p, here, :] + laplace
                       + wgt[p, here, :] * u[at_u, 1 + p, pad, :])
                hist[t + 2, p, here, :] = new
                s[later, 1 + p, pad, :] = spd[p, here, :] * new
            if k == 1:
                @pl.when(t < steps - 1)
                def _():
                    start((0, 1), s, later, a_sems(later))

        @pl.when(t < steps - 1)
        def _():
            start((2, 3), s, later, a_sems(later))
        for p in range(planes):
            for r in range(0, rows, CHUNK):
                here = slice(r, r + CHUNK)
                image[p, here, :] += hist[t + 1, p, here, :] * laps[at_lap, p, here, :]
        return carry

    def start_copy(g, d):
        return pltpu.make_async_remote_copy(
            src_ref=stage.at[g], dst_ref=st_o.at[0, :, :, mine, :],
            send_sem=st_send.at[g], recv_sem=st_recv.at[d],
            device_id={"tm": g}, device_id_type=pl.DeviceIdType.MESH)

    def own_copy(g):
        return pltpu.make_async_copy(stage.at[g], st_o.at[0, :, :, mine, :], st_send.at[g])

    def send_start(g):
        end = tab[2 * steps + groups + g]
        for p in range(planes):
            stage[g, 0, p] = hist[end + 1, p]
            stage[g, 1, p] = hist[end, p]
        for m in range(groups):
            @pl.when(me == m)
            def _():
                if m == g:
                    own_copy(g).start()
                else:
                    start_copy(g, (m - g) % groups).start()

    done = 0
    for g in reversed(range(groups)):
        until = min(steps, (groups - g) * SLAB_MAX) if g > 0 else steps
        if until > done:
            lax.fori_loop(done, until, adjoint, 0)
            done = until
        send_start(g)

    def image_copy(i):
        return pltpu.make_async_remote_copy(
            src_ref=image, dst_ref=img_o.at[:, mine, :],
            send_sem=im_send.at[i], recv_sem=im_recv.at[i],
            device_id={"tm": partners[i]}, device_id_type=pl.DeviceIdType.MESH)

    for i in range(len(partners)):
        image_copy(i).start()
    own_image = pltpu.make_async_copy(image, img_o.at[:, mine, :], load_sem.at[0])
    own_image.start()

    for i in range(len(partners)):
        ck_copy(i).wait_send()
    for g in range(groups):
        for m in range(groups):
            @pl.when(me == m)
            def _():
                if m == g:
                    own_copy(g).wait()
                    for d in range(1, groups):
                        start_copy(g, d).wait_recv()
                else:
                    start_copy(g, (m - g) % groups).wait_send()
    for i in range(len(partners)):
        image_copy(i).wait()
    own_image.wait()


def run(steps, number, speed_sq, misfit_weight, checkpoints, adjoint_final, slab_steps, restart_group):
    planes, ny, nz = speed_sq.shape
    groups = slab_steps.shape[0]
    rows = ny // groups
    f32 = jnp.float32
    ends = jnp.cumsum(slab_steps[::-1])[::-1]
    begins = ends - slab_steps
    t = jnp.arange(steps)[:, None]
    inside = (t >= begins[None]) & (t < ends[None])
    n = slab_steps[None] - (t - begins[None])
    g = jnp.arange(groups)[None]
    some = jnp.any(inside, axis=1)
    at_u = jnp.sum(jnp.where(inside, (n + 1) * groups + g, 0), axis=1)
    at_lap = jnp.where(some, jnp.sum(jnp.where(inside, (n - 1) * groups + g, 0), axis=1), SLAB_MAX * groups)
    at_u = jnp.where(some, at_u, groups)
    table = jnp.concatenate([at_u, at_lap, restart_group, ends]).astype(jnp.int32)
    anywhere = pl.BlockSpec(memory_space=pl.ANY)
    padded = (planes + 2, rows + 2 * EDGE, nz)
    block = (planes, rows, nz)
    dma = pltpu.SemaphoreType.DMA
    return pl.pallas_call(
        functools.partial(kernel, steps),
        out_shape=(jax.ShapeDtypeStruct(speed_sq.shape, f32),
                   jax.ShapeDtypeStruct((1, 2) + speed_sq.shape, f32)),
        in_specs=[pl.BlockSpec(memory_space=pltpu.SMEM)] + [anywhere] * 4,
        out_specs=(anywhere, anywhere),
        scratch_shapes=[
            pltpu.VMEM((groups, 2) + block, f32),
            pltpu.VMEM(((SLAB_MAX + 2) * groups,) + padded, f32),
            pltpu.VMEM((SLAB_MAX * groups + 1,) + block, f32),
            pltpu.VMEM((2,) + padded, f32),
            pltpu.VMEM((steps + 2,) + block, f32),
            pltpu.VMEM(block, f32),
            pltpu.VMEM(block, f32),
            pltpu.VMEM(block, f32),
            pltpu.VMEM((groups, 2) + block, f32),
            dma((5,)), dma((groups - 1,)), dma((groups - 1,)),
            dma((2, groups, 4)), dma((2, groups, 4)), dma((2, 4)), dma((2, 4)),
            dma((groups,)), dma((groups,)), dma((groups - 1,)), dma((groups - 1,)),
        ],
        compiler_params=pltpu.CompilerParams(
            collective_id=number, has_side_effects=True, vmem_limit_bytes=56 * 1024 * 1024),
        name=f"wave{steps}",
    )(table, speed_sq, misfit_weight, checkpoints, adjoint_final)


def shards(*args):
    return run(SLAB_MAX * args[4].shape[0], 0, *args)


def solution(mesh):
    placed = (
        P("space", None, None),
        P("space", None, None),
        P("tm", None, "space", None, None),
        P(None, "space", None, None),
        P(),
        P(),
    )
    return jax.shard_map(
        shards,
        mesh=mesh,
        in_specs=placed,
        out_specs=(P("space", None, None), P("tm", None, "space", None, None)),
        check_vma=False,
    )
```

```python
import functools

import jax
import jax.numpy as jnp
from jax import lax
from jax.experimental import pallas as pl
from jax.experimental.pallas import tpu as pltpu
from jax.sharding import PartitionSpec as P

SLAB_MAX = 6
CHUNK = 32
WIDE = 40
EDGE = 8


def kernel(steps, tab, speed_h, weight_h, ck_h, af_h, img_o, st_o,
           ck, u, laps, s, hist, image, spd, wgt, stage,
           yin, y_send, y_recv, load_sem, ck_send, ck_recv, f_send, f_recv, a_send, a_recv,
           st_send, st_recv, im_send, im_recv):
    groups = st_recv.shape[0]
    planes, rows, nz = image.shape
    wide = rows + 2 * EDGE
    me = lax.axis_index("tm")
    sp = lax.axis_index("space")
    n_tm = lax.axis_size("tm")
    n_sp = lax.axis_size("space")

    def place(m):
        return m + (m // 2) * (1 - 2 * (m % 2))

    q = place(me)
    inner = pl.ds(EDGE, rows)
    span = pl.ds(1, planes)
    partners = [lax.rem(me + d, n_tm) for d in range(1, n_tm)]
    has = [sp > 0, sp < n_sp - 1, q > 0, q < n_tm - 1]
    opposite = [1, 0, 3, 2]
    target = [{"space": jnp.maximum(sp - 1, 0)}, {"space": jnp.minimum(sp + 1, n_sp - 1)},
              {"tm": place(jnp.maximum(q - 1, 0))}, {"tm": place(jnp.minimum(q + 1, n_tm - 1))}]

    def halo(d, ref, at, send, recv):
        span_y = pl.ds(EDGE, ref.shape[2] - 2 * EDGE)
        if d == 0:
            src, dst = ref.at[at, 1, span_y, :], ref.at[at, planes + 1, span_y, :]
        elif d == 1:
            src, dst = ref.at[at, planes, span_y, :], ref.at[at, 0, span_y, :]
        elif d == 2:
            src, dst = ref.at[at, span, pl.ds(EDGE, EDGE), :], ref.at[at, span, pl.ds(EDGE + rows, EDGE), :]
        else:
            src, dst = ref.at[at, span, pl.ds(rows, EDGE), :], ref.at[at, span, pl.ds(0, EDGE), :]
        return pltpu.make_async_remote_copy(
            src_ref=src, dst_ref=dst, send_sem=send, recv_sem=recv,
            device_id=target[d], device_id_type=pl.DeviceIdType.MESH)

    def start(dirs, ref, at, sems):
        for d in dirs:
            @pl.when(has[d])
            def _():
                halo(d, ref, at, sems[0](d), sems[1](d)).start()

    def finish(dirs, ref, at, sems):
        for d in dirs:
            @pl.when(has[opposite[d]])
            def _():
                halo(d, ref, at, sems[0](d), sems[1](d)).wait_recv()
        for d in dirs:
            @pl.when(has[d])
            def _():
                halo(d, ref, at, sems[0](d), sems[1](d)).wait_send()

    mine = pl.ds(pl.multiple_of(q * rows, rows), rows)
    loads = [pltpu.make_async_copy(ck_h.at[0, :, :, mine, :], ck.at[me], load_sem.at[0, 0])]
    fields = [(speed_h, spd), (weight_h, wgt), (af_h.at[0], hist.at[1]), (af_h.at[1], hist.at[0])]
    below = pl.ds(pl.multiple_of(jnp.maximum(q * rows - EDGE, 0), EDGE), EDGE)
    above = pl.ds(pl.multiple_of(jnp.minimum(q * rows + rows, n_tm * rows - EDGE), EDGE), EDGE)
    edges = []
    for i, (src, dst) in enumerate(fields):
        loads.append(pltpu.make_async_copy(src.at[:, mine, :], dst.at[:, inner, :], load_sem.at[1 + i, 0]))
        edges.append((has[2], dst, 0, pltpu.make_async_copy(
            src.at[:, below, :], dst.at[:, pl.ds(0, EDGE), :], load_sem.at[1 + i, 1])))
        edges.append((has[3], dst, EDGE + rows, pltpu.make_async_copy(
            src.at[:, above, :], dst.at[:, pl.ds(EDGE + rows, EDGE), :], load_sem.at[1 + i, 2])))
    for one in loads:
        one.start()
    for there, _, _, one in edges:
        @pl.when(there)
        def _():
            one.start()

    barrier = pltpu.get_barrier_semaphore()
    for m in partners:
        pl.semaphore_signal(barrier, inc=1, device_id={"tm": m}, device_id_type=pl.DeviceIdType.MESH)
    for d in range(2):
        @pl.when(has[d])
        def _():
            pl.semaphore_signal(barrier, inc=1, device_id=target[d], device_id_type=pl.DeviceIdType.MESH)
    peers = len(partners) + has[0].astype(jnp.int32) + has[1].astype(jnp.int32)
    pl.semaphore_wait(barrier, peers)

    def ck_copy(i):
        m = partners[i]
        theirs = pl.ds(pl.multiple_of(place(m) * rows, rows), rows)
        return pltpu.make_async_remote_copy(
            src_ref=ck_h.at[0, :, :, theirs, :], dst_ref=ck.at[me],
            send_sem=ck_send.at[i], recv_sem=ck_recv.at[i],
            device_id={"tm": m}, device_id_type=pl.DeviceIdType.MESH)

    for i in range(len(partners)):
        ck_copy(i).start()

    line = jnp.zeros((rows, nz), jnp.float32)
    band = jnp.zeros((EDGE, nz), jnp.float32)
    for ref in (u, s):
        for d, p in ((0, 0), (1, planes + 1)):
            @pl.when(jnp.logical_not(has[d]))
            def _():
                def clear(i, c):
                    for r in range(EDGE, ref.shape[2] - EDGE, EDGE):
                        ref[i, p, r:r + EDGE, :] = band
                    return c
                lax.fori_loop(0, ref.shape[0], clear, 0)
    for d, r in ((2, 0), (3, EDGE + rows)):
        @pl.when(jnp.logical_not(has[d]))
        def _():
            def clear(i, c):
                for p in range(planes):
                    u[i, 1 + p, r:r + EDGE, :] = band
                return c
            lax.fori_loop(0, u.shape[0], clear, 0)
    for i in range(2):
        for p in range(planes):
            s[i, 1 + p, 0:EDGE, :] = band
            s[i, 1 + p, EDGE + wide:2 * EDGE + wide, :] = band
    for there, dst, r, _ in edges:
        @pl.when(jnp.logical_not(there))
        def _():
            for p in range(planes):
                dst[p, r:r + EDGE, :] = band
    blank = laps.shape[0] - 1
    for p in range(planes):
        laps[blank, p] = line
        image[p] = line

    def lap(ref, at, p, r, size):
        lane = lax.broadcasted_iota(jnp.int32, (size, nz), 1)
        zero = jnp.zeros((size, nz), jnp.float32)
        c = ref[at, p + 1, EDGE + r:EDGE + r + size, :]
        total = ref[at, p, EDGE + r:EDGE + r + size, :] + ref[at, p + 2, EDGE + r:EDGE + r + size, :]
        total += ref[at, p + 1, EDGE + r - 1:EDGE + r - 1 + size, :]
        total += ref[at, p + 1, EDGE + r + 1:EDGE + r + 1 + size, :]
        total += jnp.where(lane == 0, zero, pltpu.roll(c, 1, 1))
        total += jnp.where(lane == nz - 1, zero, pltpu.roll(c, nz - 1, 1))
        return c, total - 6.0 * c

    for one in loads:
        one.wait()
    for there, _, _, one in edges:
        @pl.when(there)
        def _():
            one.wait()

    def a_sems(par):
        return (lambda d: a_send.at[par, d]), (lambda d: a_recv.at[par, d])

    def f_sems(par, g):
        return (lambda d: f_send.at[par, g, d]), (lambda d: f_recv.at[par, g, d])

    for p in range(planes):
        s[0, 1 + p, EDGE:EDGE + wide, :] = spd[p] * hist[1, p]

    for i in range(len(partners)):
        ck_copy(i).wait_recv()
    for g in range(groups):
        source = tab[2 * steps + g]
        for p in range(planes):
            u[groups + g, 1 + p, EDGE:EDGE + rows, :] = ck[source, 1, p]
        start(range(4), u, groups + g, f_sems(0, g))
        for p in range(planes):
            u[g, 1 + p, EDGE:EDGE + rows, :] = ck[source, 0, p]
    start((0, 1), s, 0, a_sems(0))

    order = (0, planes - 1) + tuple(range(1, planes - 1))

    def forward(n, carry):
        par, later = lax.rem(n, 2), lax.rem(n + 1, 2)
        for g in range(groups):
            at = (n + 1) * groups + g
            finish(range(4), u, at, f_sems(par, g))
            for k, p in enumerate(order):
                for r in range(0, rows, CHUNK):
                    here = slice(EDGE + r, EDGE + r + CHUNK)
                    c, laplace = lap(u, at, p, r, CHUNK)
                    laps[n * groups + g, p, r:r + CHUNK, :] = laplace
                    u[at + groups, 1 + p, here, :] = (
                        2.0 * c - u[at - groups, 1 + p, here, :] + spd[p, here, :] * laplace)
                if k == 1:
                    @pl.when(n < SLAB_MAX - 1)
                    def _():
                        start((0, 1), u, at + groups, f_sems(later, g))

            start((2, 3), u, at + groups, f_sems(later, g))
        return carry

    lax.fori_loop(0, SLAB_MAX, forward, 0)
    for g in range(groups):
        finish((2, 3), u, (SLAB_MAX + 1) * groups + g, f_sems(SLAB_MAX % 2, g))

    def adjoint(t, carry):
        par, later = lax.rem(t, 2), lax.rem(t + 1, 2)
        at_u, at_lap = tab[t], tab[steps + t]
        finish((0, 1), s, par, a_sems(par))
        for k, p in enumerate(order):
            for r in range(0, wide, WIDE):
                here = slice(r, r + WIDE)
                pad = slice(EDGE + r, EDGE + r + WIDE)
                _, laplace = lap(s, par, p, r, WIDE)
                new = (2.0 * hist[t + 1, p, here, :] - hist[t, p, here, :] + laplace
                       + wgt[p, here, :] * u[at_u, 1 + p, here, :])
                hist[t + 2, p, here, :] = new
                s[later, 1 + p, pad, :] = spd[p, here, :] * new
            if k == 1:
                @pl.when(jnp.logical_and(t < steps - 1, lax.rem(t + 1, EDGE) != 0))
                def _():
                    start((0, 1), s, later, a_sems(later))
        for p in range(planes):
            for r in range(0, rows, CHUNK):
                here = slice(r, r + CHUNK)
                image[p, here, :] += (hist[t + 1, p, EDGE + r:EDGE + r + CHUNK, :]
                                      * laps[at_lap, p, here, :])
        return carry

    def y_copy(t, k, d):
        first = EDGE if d == 2 else rows
        return pltpu.make_async_remote_copy(
            src_ref=hist.at[pl.ds(t, 2), :, pl.ds(first, EDGE), :], dst_ref=yin.at[k, d - 2],
            send_sem=y_send.at[k, d - 2], recv_sem=y_recv.at[k, d - 2],
            device_id=target[d], device_id_type=pl.DeviceIdType.MESH)

    def refresh(t):
        k, par = t // EDGE - 1, t % 2
        for d in (2, 3):
            @pl.when(has[d])
            def _():
                y_copy(t, k, d).start()
        for d in (2, 3):
            r = 0 if d == 3 else EDGE + rows

            @pl.when(has[opposite[d]])
            def _():
                y_copy(t, k, d).wait_recv()
                for p in range(planes):
                    old, now = yin[k, d - 2, 0, p], yin[k, d - 2, 1, p]
                    hist[t, p, r:r + EDGE, :] = old
                    hist[t + 1, p, r:r + EDGE, :] = now
                    s[par, 1 + p, EDGE + r:2 * EDGE + r, :] = spd[p, r:r + EDGE, :] * now
        start((0, 1), s, par, a_sems(par))
        for d in (2, 3):
            @pl.when(has[d])
            def _():
                y_copy(t, k, d).wait_send()

    def start_copy(g, d):
        return pltpu.make_async_remote_copy(
            src_ref=stage.at[g], dst_ref=st_o.at[0, :, :, mine, :],
            send_sem=st_send.at[g], recv_sem=st_recv.at[d],
            device_id={"tm": g}, device_id_type=pl.DeviceIdType.MESH)

    def own_copy(g):
        return pltpu.make_async_copy(stage.at[g], st_o.at[0, :, :, mine, :], st_send.at[g])

    def send_start(g):
        end = tab[2 * steps + groups + g]
        for p in range(planes):
            stage[g, 0, p] = hist[end + 1, p, EDGE:EDGE + rows, :]
            stage[g, 1, p] = hist[end, p, EDGE:EDGE + rows, :]
        for m in range(groups):
            @pl.when(me == m)
            def _():
                if m == g:
                    own_copy(g).start()
                else:
                    start_copy(g, (m - g) % groups).start()

    done = 0
    for g in reversed(range(groups)):
        until = min(steps, (groups - g) * SLAB_MAX) if g > 0 else steps
        while done < until:
            stop = min(until, (done // EDGE + 1) * EDGE)
            lax.fori_loop(done, stop, adjoint, 0)
            done = stop
            if done % EDGE == 0 and done < steps:
                refresh(done)
        send_start(g)

    def image_copy(i):
        return pltpu.make_async_remote_copy(
            src_ref=image, dst_ref=img_o.at[:, mine, :],
            send_sem=im_send.at[i], recv_sem=im_recv.at[i],
            device_id={"tm": partners[i]}, device_id_type=pl.DeviceIdType.MESH)

    for i in range(len(partners)):
        image_copy(i).start()
    own_image = pltpu.make_async_copy(image, img_o.at[:, mine, :], load_sem.at[0, 0])
    own_image.start()

    for i in range(len(partners)):
        ck_copy(i).wait_send()
    for g in range(groups):
        for m in range(groups):
            @pl.when(me == m)
            def _():
                if m == g:
                    own_copy(g).wait()
                    for d in range(1, groups):
                        start_copy(g, d).wait_recv()
                else:
                    start_copy(g, (m - g) % groups).wait_send()
    for i in range(len(partners)):
        image_copy(i).wait()
    own_image.wait()


def run(steps, number, speed_sq, misfit_weight, checkpoints, adjoint_final, slab_steps, restart_group):
    planes, ny, nz = speed_sq.shape
    groups = slab_steps.shape[0]
    rows = ny // groups
    f32 = jnp.float32
    ends = jnp.cumsum(slab_steps[::-1])[::-1]
    begins = ends - slab_steps
    t = jnp.arange(steps)[:, None]
    inside = (t >= begins[None]) & (t < ends[None])
    n = slab_steps[None] - (t - begins[None])
    g = jnp.arange(groups)[None]
    some = jnp.any(inside, axis=1)
    at_u = jnp.sum(jnp.where(inside, (n + 1) * groups + g, 0), axis=1)
    at_lap = jnp.where(some, jnp.sum(jnp.where(inside, (n - 1) * groups + g, 0), axis=1), SLAB_MAX * groups)
    at_u = jnp.where(some, at_u, groups)
    table = jnp.concatenate([at_u, at_lap, restart_group, ends]).astype(jnp.int32)
    anywhere = pl.BlockSpec(memory_space=pl.ANY)
    padded = (planes + 2, rows + 2 * EDGE, nz)
    block = (planes, rows, nz)
    tall = (planes, rows + 2 * EDGE, nz)
    turns = max(1, (steps - 1) // EDGE)
    dma = pltpu.SemaphoreType.DMA
    return pl.pallas_call(
        functools.partial(kernel, steps),
        out_shape=(jax.ShapeDtypeStruct(speed_sq.shape, f32),
                   jax.ShapeDtypeStruct((1, 2) + speed_sq.shape, f32)),
        in_specs=[pl.BlockSpec(memory_space=pltpu.SMEM)] + [anywhere] * 4,
        out_specs=(anywhere, anywhere),
        scratch_shapes=[
            pltpu.VMEM((groups, 2) + block, f32),
            pltpu.VMEM(((SLAB_MAX + 2) * groups,) + padded, f32),
            pltpu.VMEM((SLAB_MAX * groups + 1,) + block, f32),
            pltpu.VMEM((2, planes + 2, rows + 4 * EDGE, nz), f32),
            pltpu.VMEM((steps + 2,) + tall, f32),
            pltpu.VMEM(block, f32),
            pltpu.VMEM(tall, f32),
            pltpu.VMEM(tall, f32),
            pltpu.VMEM((groups, 2) + block, f32),
            pltpu.VMEM((turns, 2, 2, planes, EDGE, nz), f32),
            dma((turns, 2)), dma((turns, 2)),
            dma((5, 3)), dma((groups - 1,)), dma((groups - 1,)),
            dma((2, groups, 4)), dma((2, groups, 4)), dma((2, 4)), dma((2, 4)),
            dma((groups,)), dma((groups,)), dma((groups - 1,)), dma((groups - 1,)),
        ],
        compiler_params=pltpu.CompilerParams(
            collective_id=number, has_side_effects=True, vmem_limit_bytes=56 * 1024 * 1024),
        name=f"wave{steps}",
    )(table, speed_sq, misfit_weight, checkpoints, adjoint_final)


def shards(*args):
    return run(SLAB_MAX * args[4].shape[0], 0, *args)


def solution(mesh):
    placed = (
        P("space", None, None),
        P("space", None, None),
        P("tm", None, "space", None, None),
        P(None, "space", None, None),
        P(),
        P(),
    )
    return jax.shard_map(
        shards,
        mesh=mesh,
        in_specs=placed,
        out_specs=(P("space", None, None), P("tm", None, "space", None, None)),
        check_vma=False,
    )
```

```python
import functools

import jax
import jax.numpy as jnp
from jax import lax
from jax.experimental import pallas as pl
from jax.experimental.pallas import tpu as pltpu
from jax.sharding import PartitionSpec as P

SLAB_MAX = 6
CHUNK = 32
WIDE = 40
EDGE = 8
COUNTS = (14, 16, 20)


def kernel(steps, tab, speed_h, weight_h, ck_h, af_h, img_o, st_o,
           ck, u, laps, s, hist, image, spd, wgt, stage,
           yin, y_send, y_recv, load_sem, ck_send, ck_recv, f_send, f_recv, a_send, a_recv,
           st_send, st_recv, im_send, im_recv):
    groups = st_recv.shape[0]
    planes, rows, nz = image.shape
    wide = rows + 2 * EDGE
    me = lax.axis_index("tm")
    sp = lax.axis_index("space")
    n_tm = lax.axis_size("tm")
    n_sp = lax.axis_size("space")

    def place(m):
        return m + (m // 2) * (1 - 2 * (m % 2))

    q = place(me)
    inner = pl.ds(EDGE, rows)
    span = pl.ds(1, planes)
    partners = [lax.rem(me + d, n_tm) for d in range(1, n_tm)]
    has = [sp > 0, sp < n_sp - 1, q > 0, q < n_tm - 1]
    opposite = [1, 0, 3, 2]
    target = [{"space": jnp.maximum(sp - 1, 0)}, {"space": jnp.minimum(sp + 1, n_sp - 1)},
              {"tm": place(jnp.maximum(q - 1, 0))}, {"tm": place(jnp.minimum(q + 1, n_tm - 1))}]

    def halo(d, ref, at, send, recv):
        span_y = pl.ds(EDGE, ref.shape[2] - 2 * EDGE)
        if d == 0:
            src, dst = ref.at[at, 1, span_y, :], ref.at[at, planes + 1, span_y, :]
        elif d == 1:
            src, dst = ref.at[at, planes, span_y, :], ref.at[at, 0, span_y, :]
        elif d == 2:
            src, dst = ref.at[at, span, pl.ds(EDGE, EDGE), :], ref.at[at, span, pl.ds(EDGE + rows, EDGE), :]
        else:
            src, dst = ref.at[at, span, pl.ds(rows, EDGE), :], ref.at[at, span, pl.ds(0, EDGE), :]
        return pltpu.make_async_remote_copy(
            src_ref=src, dst_ref=dst, send_sem=send, recv_sem=recv,
            device_id=target[d], device_id_type=pl.DeviceIdType.MESH)

    def start(dirs, ref, at, sems):
        for d in dirs:
            @pl.when(has[d])
            def _():
                halo(d, ref, at, sems[0](d), sems[1](d)).start()

    def finish(dirs, ref, at, sems):
        for d in dirs:
            @pl.when(has[opposite[d]])
            def _():
                halo(d, ref, at, sems[0](d), sems[1](d)).wait_recv()
        for d in dirs:
            @pl.when(has[d])
            def _():
                halo(d, ref, at, sems[0](d), sems[1](d)).wait_send()

    mine = pl.ds(pl.multiple_of(q * rows, rows), rows)
    loads = [pltpu.make_async_copy(ck_h.at[0, :, :, mine, :], ck.at[me], load_sem.at[0, 0])]
    fields = [(speed_h, spd), (weight_h, wgt), (af_h.at[0], hist.at[1]), (af_h.at[1], hist.at[0])]
    below = pl.ds(pl.multiple_of(jnp.maximum(q * rows - EDGE, 0), EDGE), EDGE)
    above = pl.ds(pl.multiple_of(jnp.minimum(q * rows + rows, n_tm * rows - EDGE), EDGE), EDGE)
    edges = []
    for i, (src, dst) in enumerate(fields):
        loads.append(pltpu.make_async_copy(src.at[:, mine, :], dst.at[:, inner, :], load_sem.at[1 + i, 0]))
        edges.append((has[2], dst, 0, pltpu.make_async_copy(
            src.at[:, below, :], dst.at[:, pl.ds(0, EDGE), :], load_sem.at[1 + i, 1])))
        edges.append((has[3], dst, EDGE + rows, pltpu.make_async_copy(
            src.at[:, above, :], dst.at[:, pl.ds(EDGE + rows, EDGE), :], load_sem.at[1 + i, 2])))
    for one in loads:
        one.start()
    for there, _, _, one in edges:
        @pl.when(there)
        def _():
            one.start()

    barrier = pltpu.get_barrier_semaphore()
    for m in partners:
        pl.semaphore_signal(barrier, inc=1, device_id={"tm": m}, device_id_type=pl.DeviceIdType.MESH)
    for d in range(2):
        @pl.when(has[d])
        def _():
            pl.semaphore_signal(barrier, inc=1, device_id=target[d], device_id_type=pl.DeviceIdType.MESH)
    peers = len(partners) + has[0].astype(jnp.int32) + has[1].astype(jnp.int32)
    pl.semaphore_wait(barrier, peers)

    def ck_copy(i):
        m = partners[i]
        theirs = pl.ds(pl.multiple_of(place(m) * rows, rows), rows)
        return pltpu.make_async_remote_copy(
            src_ref=ck_h.at[0, :, :, theirs, :], dst_ref=ck.at[me],
            send_sem=ck_send.at[i], recv_sem=ck_recv.at[i],
            device_id={"tm": m}, device_id_type=pl.DeviceIdType.MESH)

    for i in range(len(partners)):
        ck_copy(i).start()

    line = jnp.zeros((rows, nz), jnp.float32)
    band = jnp.zeros((EDGE, nz), jnp.float32)
    for ref in (u, s):
        for d, p in ((0, 0), (1, planes + 1)):
            @pl.when(jnp.logical_not(has[d]))
            def _():
                def clear(i, c):
                    for r in range(EDGE, ref.shape[2] - EDGE, EDGE):
                        ref[i, p, r:r + EDGE, :] = band
                    return c
                lax.fori_loop(0, ref.shape[0], clear, 0)
    for d, r in ((2, 0), (3, EDGE + rows)):
        @pl.when(jnp.logical_not(has[d]))
        def _():
            def clear(i, c):
                for p in range(planes):
                    u[i, 1 + p, r:r + EDGE, :] = band
                return c
            lax.fori_loop(0, u.shape[0], clear, 0)
    for i in range(2):
        for p in range(planes):
            s[i, 1 + p, 0:EDGE, :] = band
            s[i, 1 + p, EDGE + wide:2 * EDGE + wide, :] = band
    for there, dst, r, _ in edges:
        @pl.when(jnp.logical_not(there))
        def _():
            for p in range(planes):
                dst[p, r:r + EDGE, :] = band
    blank = laps.shape[0] - 1
    for p in range(planes):
        laps[blank, p] = line
        image[p] = line

    def lap(ref, at, p, r, size):
        lane = lax.broadcasted_iota(jnp.int32, (size, nz), 1)
        zero = jnp.zeros((size, nz), jnp.float32)
        c = ref[at, p + 1, EDGE + r:EDGE + r + size, :]
        total = ref[at, p, EDGE + r:EDGE + r + size, :] + ref[at, p + 2, EDGE + r:EDGE + r + size, :]
        total += ref[at, p + 1, EDGE + r - 1:EDGE + r - 1 + size, :]
        total += ref[at, p + 1, EDGE + r + 1:EDGE + r + 1 + size, :]
        total += jnp.where(lane == 0, zero, pltpu.roll(c, 1, 1))
        total += jnp.where(lane == nz - 1, zero, pltpu.roll(c, nz - 1, 1))
        return c, total - 6.0 * c

    for one in loads:
        one.wait()
    for there, _, _, one in edges:
        @pl.when(there)
        def _():
            one.wait()

    def a_sems(par):
        return (lambda d: a_send.at[par, d]), (lambda d: a_recv.at[par, d])

    def f_sems(par, g):
        return (lambda d: f_send.at[par, g, d]), (lambda d: f_recv.at[par, g, d])

    for p in range(planes):
        s[0, 1 + p, EDGE:EDGE + wide, :] = spd[p] * hist[1, p]

    for i in range(len(partners)):
        ck_copy(i).wait_recv()
    for g in range(groups):
        source = tab[2 * steps + g]
        for p in range(planes):
            u[groups + g, 1 + p, EDGE:EDGE + rows, :] = ck[source, 1, p]
        start(range(4), u, groups + g, f_sems(0, g))
        for p in range(planes):
            u[g, 1 + p, EDGE:EDGE + rows, :] = ck[source, 0, p]
    start((0, 1), s, 0, a_sems(0))

    order = (0, planes - 1) + tuple(range(1, planes - 1))

    def forward(n, carry):
        par, later = lax.rem(n, 2), lax.rem(n + 1, 2)
        for g in range(groups):
            at = (n + 1) * groups + g
            finish(range(4), u, at, f_sems(par, g))
            for k, p in enumerate(order):
                for r in range(0, rows, CHUNK):
                    here = slice(EDGE + r, EDGE + r + CHUNK)
                    c, laplace = lap(u, at, p, r, CHUNK)
                    laps[n * groups + g, p, r:r + CHUNK, :] = laplace
                    u[at + groups, 1 + p, here, :] = (
                        2.0 * c - u[at - groups, 1 + p, here, :] + spd[p, here, :] * laplace)
                if k == 1:
                    @pl.when(n < SLAB_MAX - 1)
                    def _():
                        start((0, 1), u, at + groups, f_sems(later, g))

            start((2, 3), u, at + groups, f_sems(later, g))
        return carry

    lax.fori_loop(0, SLAB_MAX, forward, 0)
    for g in range(groups):
        finish((2, 3), u, (SLAB_MAX + 1) * groups + g, f_sems(SLAB_MAX % 2, g))

    def adjoint(t, carry):
        par, later = lax.rem(t, 2), lax.rem(t + 1, 2)
        at_u, at_lap = tab[t], tab[steps + t]
        finish((0, 1), s, par, a_sems(par))
        for k, p in enumerate(order):
            for r in range(0, wide, WIDE):
                here = slice(r, r + WIDE)
                pad = slice(EDGE + r, EDGE + r + WIDE)
                _, laplace = lap(s, par, p, r, WIDE)
                new = (2.0 * hist[t + 1, p, here, :] - hist[t, p, here, :] + laplace
                       + wgt[p, here, :] * u[at_u, 1 + p, here, :])
                hist[t + 2, p, here, :] = new
                s[later, 1 + p, pad, :] = spd[p, here, :] * new
            if k == 1:
                @pl.when(jnp.logical_and(t < steps - 1, lax.rem(t + 1, EDGE) != 0))
                def _():
                    start((0, 1), s, later, a_sems(later))
        for p in range(planes):
            for r in range(0, rows, CHUNK):
                here = slice(r, r + CHUNK)
                image[p, here, :] += (hist[t + 1, p, EDGE + r:EDGE + r + CHUNK, :]
                                      * laps[at_lap, p, here, :])
        return carry

    def y_copy(t, k, d):
        first = EDGE if d == 2 else rows
        return pltpu.make_async_remote_copy(
            src_ref=hist.at[pl.ds(t, 2), :, pl.ds(first, EDGE), :], dst_ref=yin.at[k, d - 2],
            send_sem=y_send.at[k, d - 2], recv_sem=y_recv.at[k, d - 2],
            device_id=target[d], device_id_type=pl.DeviceIdType.MESH)

    def refresh(t):
        k, par = t // EDGE - 1, t % 2
        for d in (2, 3):
            @pl.when(has[d])
            def _():
                y_copy(t, k, d).start()
        for d in (2, 3):
            r = 0 if d == 3 else EDGE + rows

            @pl.when(has[opposite[d]])
            def _():
                y_copy(t, k, d).wait_recv()
                for p in range(planes):
                    old, now = yin[k, d - 2, 0, p], yin[k, d - 2, 1, p]
                    hist[t, p, r:r + EDGE, :] = old
                    hist[t + 1, p, r:r + EDGE, :] = now
                    s[par, 1 + p, EDGE + r:2 * EDGE + r, :] = spd[p, r:r + EDGE, :] * now
        start((0, 1), s, par, a_sems(par))
        for d in (2, 3):
            @pl.when(has[d])
            def _():
                y_copy(t, k, d).wait_send()

    def start_copy(g, d):
        return pltpu.make_async_remote_copy(
            src_ref=stage.at[g], dst_ref=st_o.at[0, :, :, mine, :],
            send_sem=st_send.at[g], recv_sem=st_recv.at[d],
            device_id={"tm": g}, device_id_type=pl.DeviceIdType.MESH)

    def own_copy(g):
        return pltpu.make_async_copy(stage.at[g], st_o.at[0, :, :, mine, :], st_send.at[g])

    def send_start(g):
        end = tab[2 * steps + groups + g]
        for p in range(planes):
            stage[g, 0, p] = hist[end + 1, p, EDGE:EDGE + rows, :]
            stage[g, 1, p] = hist[end, p, EDGE:EDGE + rows, :]
        for m in range(groups):
            @pl.when(me == m)
            def _():
                if m == g:
                    own_copy(g).start()
                else:
                    start_copy(g, (m - g) % groups).start()

    done = 0
    for g in reversed(range(groups)):
        until = min(steps, (groups - g) * SLAB_MAX) if g > 0 else steps
        while done < until:
            stop = min(until, (done // EDGE + 1) * EDGE)
            lax.fori_loop(done, stop, adjoint, 0)
            done = stop
            if done % EDGE == 0 and done < steps:
                refresh(done)
        send_start(g)

    def image_copy(i):
        return pltpu.make_async_remote_copy(
            src_ref=image, dst_ref=img_o.at[:, mine, :],
            send_sem=im_send.at[i], recv_sem=im_recv.at[i],
            device_id={"tm": partners[i]}, device_id_type=pl.DeviceIdType.MESH)

    for i in range(len(partners)):
        image_copy(i).start()
    own_image = pltpu.make_async_copy(image, img_o.at[:, mine, :], load_sem.at[0, 0])
    own_image.start()

    for i in range(len(partners)):
        ck_copy(i).wait_send()
    for g in range(groups):
        for m in range(groups):
            @pl.when(me == m)
            def _():
                if m == g:
                    own_copy(g).wait()
                    for d in range(1, groups):
                        start_copy(g, d).wait_recv()
                else:
                    start_copy(g, (m - g) % groups).wait_send()
    for i in range(len(partners)):
        image_copy(i).wait()
    own_image.wait()


def run(steps, number, speed_sq, misfit_weight, checkpoints, adjoint_final, slab_steps, restart_group):
    planes, ny, nz = speed_sq.shape
    groups = slab_steps.shape[0]
    rows = ny // groups
    f32 = jnp.float32
    ends = jnp.cumsum(slab_steps[::-1])[::-1]
    begins = ends - slab_steps
    t = jnp.arange(steps)[:, None]
    inside = (t >= begins[None]) & (t < ends[None])
    n = slab_steps[None] - (t - begins[None])
    g = jnp.arange(groups)[None]
    some = jnp.any(inside, axis=1)
    at_u = jnp.sum(jnp.where(inside, (n + 1) * groups + g, 0), axis=1)
    at_lap = jnp.where(some, jnp.sum(jnp.where(inside, (n - 1) * groups + g, 0), axis=1), SLAB_MAX * groups)
    at_u = jnp.where(some, at_u, groups)
    table = jnp.concatenate([at_u, at_lap, restart_group, ends]).astype(jnp.int32)
    anywhere = pl.BlockSpec(memory_space=pl.ANY)
    padded = (planes + 2, rows + 2 * EDGE, nz)
    block = (planes, rows, nz)
    tall = (planes, rows + 2 * EDGE, nz)
    turns = max(1, (steps - 1) // EDGE)
    dma = pltpu.SemaphoreType.DMA
    return pl.pallas_call(
        functools.partial(kernel, steps),
        out_shape=(jax.ShapeDtypeStruct(speed_sq.shape, f32),
                   jax.ShapeDtypeStruct((1, 2) + speed_sq.shape, f32)),
        in_specs=[pl.BlockSpec(memory_space=pltpu.SMEM)] + [anywhere] * 4,
        out_specs=(anywhere, anywhere),
        scratch_shapes=[
            pltpu.VMEM((groups, 2) + block, f32),
            pltpu.VMEM(((SLAB_MAX + 2) * groups,) + padded, f32),
            pltpu.VMEM((SLAB_MAX * groups + 1,) + block, f32),
            pltpu.VMEM((2, planes + 2, rows + 4 * EDGE, nz), f32),
            pltpu.VMEM((steps + 2,) + tall, f32),
            pltpu.VMEM(block, f32),
            pltpu.VMEM(tall, f32),
            pltpu.VMEM(tall, f32),
            pltpu.VMEM((groups, 2) + block, f32),
            pltpu.VMEM((turns, 2, 2, planes, EDGE, nz), f32),
            dma((turns, 2)), dma((turns, 2)),
            dma((5, 3)), dma((groups - 1,)), dma((groups - 1,)),
            dma((2, groups, 4)), dma((2, groups, 4)), dma((2, 4)), dma((2, 4)),
            dma((groups,)), dma((groups,)), dma((groups - 1,)), dma((groups - 1,)),
        ],
        compiler_params=pltpu.CompilerParams(
            collective_id=number, has_side_effects=True, vmem_limit_bytes=56 * 1024 * 1024),
        name=f"wave{steps}",
    )(table, speed_sq, misfit_weight, checkpoints, adjoint_final)


def shards(*args):
    full = SLAB_MAX * args[4].shape[0]
    counts = [c for c in COUNTS if c < full] + [full]
    needed = jnp.sum(args[4])
    branch = sum((needed > c).astype(jnp.int32) for c in counts[:-1])
    return lax.switch(branch, [functools.partial(run, c, i) for i, c in enumerate(counts)], *args)


def solution(mesh):
    placed = (
        P("space", None, None),
        P("space", None, None),
        P("tm", None, "space", None, None),
        P(None, "space", None, None),
        P(),
        P(),
    )
    return jax.shard_map(
        shards,
        mesh=mesh,
        in_specs=placed,
        out_specs=(P("space", None, None), P("tm", None, "space", None, None)),
        check_vma=False,
    )
```

```python
import functools

import jax
import jax.numpy as jnp
from jax import lax
from jax.experimental import pallas as pl
from jax.experimental.pallas import tpu as pltpu
from jax.sharding import PartitionSpec as P

SLAB_MAX = 6
CHUNK = 32
WIDE = 40
EDGE = 8
COUNTS = (14, 16, 20)


def kernel(steps, slab, group, speed_h, weight_h, ck_h, af_h, img_o, st_o,
           ck, u, laps, s, hist, image, spd, wgt, stage,
           yin, y_send, y_recv, load_sem, ck_send, ck_recv, f_send, f_recv, a_send, a_recv,
           st_send, st_recv, im_send, im_recv):
    groups = st_recv.shape[0]
    planes, rows, nz = image.shape
    wide = rows + 2 * EDGE
    me = lax.axis_index("tm")
    sp = lax.axis_index("space")
    n_tm = lax.axis_size("tm")
    n_sp = lax.axis_size("space")

    def place(m):
        return m + (m // 2) * (1 - 2 * (m % 2))

    q = place(me)
    inner = pl.ds(EDGE, rows)
    span = pl.ds(1, planes)
    partners = [lax.rem(me + d, n_tm) for d in range(1, n_tm)]
    has = [sp > 0, sp < n_sp - 1, q > 0, q < n_tm - 1]
    opposite = [1, 0, 3, 2]
    target = [{"space": jnp.maximum(sp - 1, 0)}, {"space": jnp.minimum(sp + 1, n_sp - 1)},
              {"tm": place(jnp.maximum(q - 1, 0))}, {"tm": place(jnp.minimum(q + 1, n_tm - 1))}]

    def halo(d, ref, at, send, recv):
        span_y = pl.ds(EDGE, ref.shape[2] - 2 * EDGE)
        if d == 0:
            src, dst = ref.at[at, 1, span_y, :], ref.at[at, planes + 1, span_y, :]
        elif d == 1:
            src, dst = ref.at[at, planes, span_y, :], ref.at[at, 0, span_y, :]
        elif d == 2:
            src, dst = ref.at[at, span, pl.ds(EDGE, EDGE), :], ref.at[at, span, pl.ds(EDGE + rows, EDGE), :]
        else:
            src, dst = ref.at[at, span, pl.ds(rows, EDGE), :], ref.at[at, span, pl.ds(0, EDGE), :]
        return pltpu.make_async_remote_copy(
            src_ref=src, dst_ref=dst, send_sem=send, recv_sem=recv,
            device_id=target[d], device_id_type=pl.DeviceIdType.MESH)

    def start(dirs, ref, at, sems):
        for d in dirs:
            @pl.when(has[d])
            def _():
                halo(d, ref, at, sems[0](d), sems[1](d)).start()

    def finish(dirs, ref, at, sems):
        for d in dirs:
            @pl.when(has[opposite[d]])
            def _():
                halo(d, ref, at, sems[0](d), sems[1](d)).wait_recv()
        for d in dirs:
            @pl.when(has[d])
            def _():
                halo(d, ref, at, sems[0](d), sems[1](d)).wait_send()

    mine = pl.ds(pl.multiple_of(q * rows, rows), rows)
    loads = [pltpu.make_async_copy(ck_h.at[0, :, :, mine, :], ck.at[me], load_sem.at[0, 0])]
    fields = [(speed_h, spd), (weight_h, wgt), (af_h.at[0], hist.at[1]), (af_h.at[1], hist.at[0])]
    below = pl.ds(pl.multiple_of(jnp.maximum(q * rows - EDGE, 0), EDGE), EDGE)
    above = pl.ds(pl.multiple_of(jnp.minimum(q * rows + rows, n_tm * rows - EDGE), EDGE), EDGE)
    edges = []
    for i, (src, dst) in enumerate(fields):
        loads.append(pltpu.make_async_copy(src.at[:, mine, :], dst.at[:, inner, :], load_sem.at[1 + i, 0]))
        edges.append((has[2], dst, 0, pltpu.make_async_copy(
            src.at[:, below, :], dst.at[:, pl.ds(0, EDGE), :], load_sem.at[1 + i, 1])))
        edges.append((has[3], dst, EDGE + rows, pltpu.make_async_copy(
            src.at[:, above, :], dst.at[:, pl.ds(EDGE + rows, EDGE), :], load_sem.at[1 + i, 2])))
    for one in loads:
        one.start()
    for there, _, _, one in edges:
        @pl.when(there)
        def _():
            one.start()

    barrier = pltpu.get_barrier_semaphore()
    for m in partners:
        pl.semaphore_signal(barrier, inc=1, device_id={"tm": m}, device_id_type=pl.DeviceIdType.MESH)
    for d in range(2):
        @pl.when(has[d])
        def _():
            pl.semaphore_signal(barrier, inc=1, device_id=target[d], device_id_type=pl.DeviceIdType.MESH)
    peers = len(partners) + has[0].astype(jnp.int32) + has[1].astype(jnp.int32)
    pl.semaphore_wait(barrier, peers)

    def ck_copy(i):
        m = partners[i]
        theirs = pl.ds(pl.multiple_of(place(m) * rows, rows), rows)
        return pltpu.make_async_remote_copy(
            src_ref=ck_h.at[0, :, :, theirs, :], dst_ref=ck.at[me],
            send_sem=ck_send.at[i], recv_sem=ck_recv.at[i],
            device_id={"tm": m}, device_id_type=pl.DeviceIdType.MESH)

    for i in range(len(partners)):
        ck_copy(i).start()

    line = jnp.zeros((rows, nz), jnp.float32)
    band = jnp.zeros((EDGE, nz), jnp.float32)
    for ref in (u, s):
        for d, p in ((0, 0), (1, planes + 1)):
            @pl.when(jnp.logical_not(has[d]))
            def _():
                def clear(i, c):
                    for r in range(EDGE, ref.shape[2] - EDGE, EDGE):
                        ref[i, p, r:r + EDGE, :] = band
                    return c
                lax.fori_loop(0, ref.shape[0], clear, 0)
    for d, r in ((2, 0), (3, EDGE + rows)):
        @pl.when(jnp.logical_not(has[d]))
        def _():
            def clear(i, c):
                for p in range(planes):
                    u[i, 1 + p, r:r + EDGE, :] = band
                return c
            lax.fori_loop(0, u.shape[0], clear, 0)
    for i in range(2):
        for p in range(planes):
            s[i, 1 + p, 0:EDGE, :] = band
            s[i, 1 + p, EDGE + wide:2 * EDGE + wide, :] = band
    for there, dst, r, _ in edges:
        @pl.when(jnp.logical_not(there))
        def _():
            for p in range(planes):
                dst[p, r:r + EDGE, :] = band
    blank = laps.shape[0] - 1
    for p in range(planes):
        laps[blank, p] = line
        image[p] = line

    def lap(ref, at, p, r, size):
        lane = lax.broadcasted_iota(jnp.int32, (size, nz), 1)
        zero = jnp.zeros((size, nz), jnp.float32)
        c = ref[at, p + 1, EDGE + r:EDGE + r + size, :]
        total = ref[at, p, EDGE + r:EDGE + r + size, :] + ref[at, p + 2, EDGE + r:EDGE + r + size, :]
        total += ref[at, p + 1, EDGE + r - 1:EDGE + r - 1 + size, :]
        total += ref[at, p + 1, EDGE + r + 1:EDGE + r + 1 + size, :]
        total += jnp.where(lane == 0, zero, pltpu.roll(c, 1, 1))
        total += jnp.where(lane == nz - 1, zero, pltpu.roll(c, nz - 1, 1))
        return c, total - 6.0 * c

    for one in loads:
        one.wait()
    for there, _, _, one in edges:
        @pl.when(there)
        def _():
            one.wait()

    def a_sems(par):
        return (lambda d: a_send.at[par, d]), (lambda d: a_recv.at[par, d])

    def f_sems(par, g):
        return (lambda d: f_send.at[par, g, d]), (lambda d: f_recv.at[par, g, d])

    for p in range(planes):
        s[0, 1 + p, EDGE:EDGE + wide, :] = spd[p] * hist[1, p]

    for i in range(len(partners)):
        ck_copy(i).wait_recv()
    for g in range(groups):
        source = group[g]
        for p in range(planes):
            u[groups + g, 1 + p, EDGE:EDGE + rows, :] = ck[source, 1, p]
        start(range(4), u, groups + g, f_sems(0, g))
        for p in range(planes):
            u[g, 1 + p, EDGE:EDGE + rows, :] = ck[source, 0, p]
    start((0, 1), s, 0, a_sems(0))

    order = (0, planes - 1) + tuple(range(1, planes - 1))

    def forward(n, carry):
        par, later = lax.rem(n, 2), lax.rem(n + 1, 2)
        for g in range(groups):
            at = (n + 1) * groups + g
            finish(range(4), u, at, f_sems(par, g))
            for k, p in enumerate(order):
                for r in range(0, rows, CHUNK):
                    here = slice(EDGE + r, EDGE + r + CHUNK)
                    c, laplace = lap(u, at, p, r, CHUNK)
                    laps[n * groups + g, p, r:r + CHUNK, :] = laplace
                    u[at + groups, 1 + p, here, :] = (
                        2.0 * c - u[at - groups, 1 + p, here, :] + spd[p, here, :] * laplace)
                if k == 1:
                    @pl.when(n < SLAB_MAX - 1)
                    def _():
                        start((0, 1), u, at + groups, f_sems(later, g))

            start((2, 3), u, at + groups, f_sems(later, g))
        return carry

    lax.fori_loop(0, SLAB_MAX, forward, 0)
    for g in range(groups):
        finish((2, 3), u, (SLAB_MAX + 1) * groups + g, f_sems(SLAB_MAX % 2, g))

    def adjoint(t, carry):
        par, later = lax.rem(t, 2), lax.rem(t + 1, 2)
        at_u, at_lap, end = jnp.int32(groups), jnp.int32(blank), jnp.int32(0)
        for g in reversed(range(groups)):
            begin, end = end, end + slab[g]
            inside = jnp.logical_and(t >= begin, t < end)
            n = end - t
            at_u = jnp.where(inside, (n + 1) * groups + g, at_u)
            at_lap = jnp.where(inside, (n - 1) * groups + g, at_lap)
        finish((0, 1), s, par, a_sems(par))
        for k, p in enumerate(order):
            for r in range(0, wide, WIDE):
                here = slice(r, r + WIDE)
                pad = slice(EDGE + r, EDGE + r + WIDE)
                _, laplace = lap(s, par, p, r, WIDE)
                new = (2.0 * hist[t + 1, p, here, :] - hist[t, p, here, :] + laplace
                       + wgt[p, here, :] * u[at_u, 1 + p, here, :])
                hist[t + 2, p, here, :] = new
                s[later, 1 + p, pad, :] = spd[p, here, :] * new
            if k == 1:
                @pl.when(jnp.logical_and(t < steps - 1, lax.rem(t + 1, EDGE) != 0))
                def _():
                    start((0, 1), s, later, a_sems(later))
        for p in range(planes):
            for r in range(0, rows, CHUNK):
                here = slice(r, r + CHUNK)
                image[p, here, :] += (hist[t + 1, p, EDGE + r:EDGE + r + CHUNK, :]
                                      * laps[at_lap, p, here, :])
        return carry

    def y_copy(t, k, d):
        first = EDGE if d == 2 else rows
        return pltpu.make_async_remote_copy(
            src_ref=hist.at[pl.ds(t, 2), :, pl.ds(first, EDGE), :], dst_ref=yin.at[k, d - 2],
            send_sem=y_send.at[k, d - 2], recv_sem=y_recv.at[k, d - 2],
            device_id=target[d], device_id_type=pl.DeviceIdType.MESH)

    def refresh(t):
        k, par = t // EDGE - 1, t % 2
        for d in (2, 3):
            @pl.when(has[d])
            def _():
                y_copy(t, k, d).start()
        for d in (2, 3):
            r = 0 if d == 3 else EDGE + rows

            @pl.when(has[opposite[d]])
            def _():
                y_copy(t, k, d).wait_recv()
                for p in range(planes):
                    old, now = yin[k, d - 2, 0, p], yin[k, d - 2, 1, p]
                    hist[t, p, r:r + EDGE, :] = old
                    hist[t + 1, p, r:r + EDGE, :] = now
                    s[par, 1 + p, EDGE + r:2 * EDGE + r, :] = spd[p, r:r + EDGE, :] * now
        start((0, 1), s, par, a_sems(par))
        for d in (2, 3):
            @pl.when(has[d])
            def _():
                y_copy(t, k, d).wait_send()

    def start_copy(g, d):
        return pltpu.make_async_remote_copy(
            src_ref=stage.at[g], dst_ref=st_o.at[0, :, :, mine, :],
            send_sem=st_send.at[g], recv_sem=st_recv.at[d],
            device_id={"tm": g}, device_id_type=pl.DeviceIdType.MESH)

    def own_copy(g):
        return pltpu.make_async_copy(stage.at[g], st_o.at[0, :, :, mine, :], st_send.at[g])

    def send_start(g):
        end = sum(slab[i] for i in range(g, groups))
        for p in range(planes):
            stage[g, 0, p] = hist[end + 1, p, EDGE:EDGE + rows, :]
            stage[g, 1, p] = hist[end, p, EDGE:EDGE + rows, :]
        for m in range(groups):
            @pl.when(me == m)
            def _():
                if m == g:
                    own_copy(g).start()
                else:
                    start_copy(g, (m - g) % groups).start()

    done = 0
    for g in reversed(range(groups)):
        until = min(steps, (groups - g) * SLAB_MAX) if g > 0 else steps
        while done < until:
            stop = min(until, (done // EDGE + 1) * EDGE)
            lax.fori_loop(done, stop, adjoint, 0)
            done = stop
            if done % EDGE == 0 and done < steps:
                refresh(done)
        send_start(g)

    def image_copy(i):
        return pltpu.make_async_remote_copy(
            src_ref=image, dst_ref=img_o.at[:, mine, :],
            send_sem=im_send.at[i], recv_sem=im_recv.at[i],
            device_id={"tm": partners[i]}, device_id_type=pl.DeviceIdType.MESH)

    for i in range(len(partners)):
        image_copy(i).start()
    own_image = pltpu.make_async_copy(image, img_o.at[:, mine, :], load_sem.at[0, 0])
    own_image.start()

    for i in range(len(partners)):
        ck_copy(i).wait_send()
    for g in range(groups):
        for m in range(groups):
            @pl.when(me == m)
            def _():
                if m == g:
                    own_copy(g).wait()
                    for d in range(1, groups):
                        start_copy(g, d).wait_recv()
                else:
                    start_copy(g, (m - g) % groups).wait_send()
    for i in range(len(partners)):
        image_copy(i).wait()
    own_image.wait()


def run(steps, number, speed_sq, misfit_weight, checkpoints, adjoint_final, slab_steps, restart_group):
    planes, ny, nz = speed_sq.shape
    groups = slab_steps.shape[0]
    rows = ny // groups
    f32 = jnp.float32
    anywhere = pl.BlockSpec(memory_space=pl.ANY)
    padded = (planes + 2, rows + 2 * EDGE, nz)
    block = (planes, rows, nz)
    tall = (planes, rows + 2 * EDGE, nz)
    turns = max(1, (steps - 1) // EDGE)
    dma = pltpu.SemaphoreType.DMA
    return pl.pallas_call(
        functools.partial(kernel, steps),
        out_shape=(jax.ShapeDtypeStruct(speed_sq.shape, f32),
                   jax.ShapeDtypeStruct((1, 2) + speed_sq.shape, f32)),
        in_specs=[pl.BlockSpec(memory_space=pltpu.SMEM)] * 2 + [anywhere] * 4,
        out_specs=(anywhere, anywhere),
        scratch_shapes=[
            pltpu.VMEM((groups, 2) + block, f32),
            pltpu.VMEM(((SLAB_MAX + 2) * groups,) + padded, f32),
            pltpu.VMEM((SLAB_MAX * groups + 1,) + block, f32),
            pltpu.VMEM((2, planes + 2, rows + 4 * EDGE, nz), f32),
            pltpu.VMEM((steps + 2,) + tall, f32),
            pltpu.VMEM(block, f32),
            pltpu.VMEM(tall, f32),
            pltpu.VMEM(tall, f32),
            pltpu.VMEM((groups, 2) + block, f32),
            pltpu.VMEM((turns, 2, 2, planes, EDGE, nz), f32),
            dma((turns, 2)), dma((turns, 2)),
            dma((5, 3)), dma((groups - 1,)), dma((groups - 1,)),
            dma((2, groups, 4)), dma((2, groups, 4)), dma((2, 4)), dma((2, 4)),
            dma((groups,)), dma((groups,)), dma((groups - 1,)), dma((groups - 1,)),
        ],
        compiler_params=pltpu.CompilerParams(
            collective_id=number, has_side_effects=True, vmem_limit_bytes=56 * 1024 * 1024),
        name=f"wave{steps}",
    )(slab_steps, restart_group, speed_sq, misfit_weight, checkpoints, adjoint_final)


def shards(*args):
    full = SLAB_MAX * args[4].shape[0]
    counts = [c for c in COUNTS if c < full] + [full]
    needed = jnp.sum(args[4])
    branch = sum((needed > c).astype(jnp.int32) for c in counts[:-1])
    return lax.switch(branch, [functools.partial(run, c, i) for i, c in enumerate(counts)], *args)


def solution(mesh):
    placed = (
        P("space", None, None),
        P("space", None, None),
        P("tm", None, "space", None, None),
        P(None, "space", None, None),
        P(),
        P(),
    )
    return jax.shard_map(
        shards,
        mesh=mesh,
        in_specs=placed,
        out_specs=(P("space", None, None), P("tm", None, "space", None, None)),
        check_vma=False,
    )
```
